32 devices in a mesh: row: 8 (over z, y), col: 4 (over x, core).
Axes of the slice: x: 2, y: 2, z: 4, core: 2. Of those that a mesh axis runs over, the one named last changes fastest.
Arguments:
- features: bfloat16 [8192, 128], P(('col', 'row')), may hold values from -6 to 6
- weight: bfloat16 [128, 256], replicated, may hold values from -0.5 to 0.5
- bias: float32 [256], replicated, may hold values from -3 to 3
- grad_out: bfloat16 [8192, 256], P(('row', 'col')), may hold values from -6 to 6
- tile_values: bfloat16 [8, 4, 128, 128, 128], P('row', 'col'), may hold values from -0.1875 to 0.1875
- tile_rows: int32 [8, 4, 128], P('row', 'col'), may hold values from 0 to 7
- tile_cols: int32 [8, 4, 128], P('row', 'col'), may hold values from 0 to 15
- tile_count: int32 [8, 4], P('row', 'col'), may hold values from 42 to 128, as said below
Outputs:
- hidden: bfloat16 [8192, 256], P(('row', 'col'))
- grad_weight: float32 [128, 256], replicated
- grad_bias: float32 [256], replicated
- grad_features: bfloat16 [8192, 128], P(('col', 'row'))
The draws below stay inside these ranges and needn't reach their ends.
Inputs may be any that keep to these rules, and one draw needn't show every extreme that they name: `tile_count`: slots below the count are live; some block has all 128 slots live.
All inputs are finite; a program needn't handle non-finite values.
Results may differ from the reference program's by a relative error of at most 0.03.
Values may be sent and summed in bfloat16 or wider, within the bound.
No kernel may reach another device: no remote copies, remote signals or barrier semaphores. Data moves between devices by JAX's collectives and lax.ppermute only.
A program may use at most 64 MiB of HBM per device.

```python
import jax
import jax.numpy as jnp
from jax import lax

F_IN = 128
HID = 256
TILE = 128
NODE_DEV = 256
KT = 128
NODES = 8192
N_ROW = 8
N_COL = 4


def draw_tile_count(key, part):
    key = jax.random.fold_in(key, 11)
    first_key, second_key = jax.random.split(key)
    counts = jax.random.randint(first_key, (N_ROW * N_COL,), KT // 3, KT + 1)
    chosen = jax.random.randint(second_key, (), 0, N_ROW * N_COL)
    counts = counts.at[chosen].set(KT)
    return counts.reshape(N_ROW, N_COL).astype(jnp.int32)


def plant(drawn, key, smallest, high):
    shape = drawn.shape
    spot = [jax.random.randint(jax.random.fold_in(key, axis), (), 0, shape[axis]) for axis in range(len(shape))]
    drawn = drawn.at[tuple(spot)].set(smallest)
    longest = shape.index(max(shape))
    spot[longest] = (spot[longest] + 1) % shape[longest]
    return drawn.at[tuple(spot)].set(high)


def level_of(stream_key, shape, cuts, smallest, high):
    gain = 1.0
    for axis_at, blocks in cuts:
        draws = jax.random.uniform(jax.random.fold_in(jax.random.fold_in(stream_key, 6), axis_at), (blocks,), jnp.float32, smallest / len(cuts), high / len(cuts))
        gain = gain * jnp.repeat(jnp.exp(draws), shape[axis_at] // blocks).reshape((-1,) + (1,) * (len(shape) - 1 - axis_at))
    return gain


def gaussian(stream_key, shape, width, reach, shards=(), held_as=jnp.bfloat16):
    drawn = width * jax.random.normal(stream_key, shape, jnp.float32)
    if shards:
        drawn = drawn * level_of(stream_key, shape, shards, -0.22, 0.18)
    return jnp.clip(drawn, -reach, reach).astype(held_as)


def setup_inputs(seed: int = 0) -> dict:
    seeds = jax.random.split(jax.random.key(seed), 9)
    return {
        "features": gaussian(seeds[0], (NODES, F_IN), 1.0, 6.0, ((0, 32),)),
        "weight": gaussian(seeds[1], (F_IN, HID), F_IN ** -0.5, 0.5),
        "bias": gaussian(seeds[2], (HID,), 0.5, 3.0, (), jnp.float32),
        "grad_out": gaussian(seeds[3], (NODES, HID), 1.0, 6.0, ((0, 32),)),
        "tile_values": gaussian(seeds[4], (N_ROW, N_COL, KT, TILE, TILE), ((0.67 * KT * TILE * TILE / NODE_DEV) ** -0.5), 0.1875, ((0, 8), (1, 4))),
        "tile_rows": plant(jax.random.randint(seeds[5], (N_ROW, N_COL, KT), 0, NODE_DEV * N_COL // TILE), jax.random.fold_in(seeds[5], 1), 0, (NODE_DEV * N_COL // TILE) - 1).astype(jnp.int32),
        "tile_cols": plant(jax.random.randint(seeds[6], (N_ROW, N_COL, KT), 0, NODE_DEV * N_ROW // TILE), jax.random.fold_in(seeds[6], 1), 0, (NODE_DEV * N_ROW // TILE) - 1).astype(jnp.int32),
        "tile_count": draw_tile_count(jax.random.fold_in(seeds[8], 71), 0),
    }


def rounded(values):
    return lax.optimization_barrier(values.astype(jnp.bfloat16)).astype(jnp.float32)


def reference(features, weight, bias, grad_out, tile_values, tile_rows, tile_cols, tile_count):
    row_tiles = NODE_DEV * N_COL // TILE
    col_tiles = NODE_DEV * N_ROW // TILE
    blocks = N_ROW * N_COL
    flat_values = tile_values.reshape(blocks, KT, TILE, TILE)
    flat_rows = tile_rows.reshape(blocks, KT)
    flat_cols = tile_cols.reshape(blocks, KT)
    flat_count = tile_count.reshape(blocks)
    slot_ids = jnp.arange(KT, dtype=jnp.int32)
    feature_tiles = features.reshape(N_COL * col_tiles, TILE, F_IN)

    def forward_step(carry, block_id):
        r_index = (block_id // N_COL).astype(jnp.int32)
        c_index = (block_id % N_COL).astype(jnp.int32)
        live = (slot_ids < flat_count[block_id]).astype(jnp.float32)
        values = flat_values[block_id].astype(jnp.float32) * live[:, None, None]
        picked = feature_tiles[c_index * col_tiles + flat_cols[block_id]].astype(jnp.float32)
        products = jnp.einsum("kij,kjf->kif", values, picked)
        summed = jax.ops.segment_sum(products, flat_rows[block_id], num_segments=row_tiles)
        start = (r_index * row_tiles).astype(jnp.int32)
        current = lax.dynamic_slice_in_dim(carry, start, row_tiles, 0)
        carry = lax.dynamic_update_slice_in_dim(carry, current + rounded(summed), start, 0)
        return carry, None

    init = jnp.zeros((N_ROW * row_tiles, TILE, F_IN), jnp.float32)
    summed_all, _ = lax.scan(forward_step, init, jnp.arange(blocks, dtype=jnp.int32))
    aggregate = summed_all.reshape(NODES, F_IN).astype(jnp.bfloat16)
    preact = jnp.dot(aggregate, weight, preferred_element_type=jnp.float32) + bias
    sigmoid_pre = jax.nn.sigmoid(preact)
    hidden = (preact * sigmoid_pre).astype(jnp.bfloat16)
    slope_factor = sigmoid_pre * (1.0 + preact * (1.0 - sigmoid_pre))
    grad_pre = (grad_out.astype(jnp.float32) * slope_factor).astype(jnp.bfloat16)
    grad_weight = jnp.dot(aggregate.T, grad_pre, preferred_element_type=jnp.float32)
    grad_bias = jnp.sum(grad_pre.astype(jnp.float32), axis=0)
    grad_aggregate = jnp.dot(grad_pre, weight.T, preferred_element_type=jnp.float32).astype(jnp.bfloat16)
    grad_tiles = grad_aggregate.reshape(N_ROW * row_tiles, TILE, F_IN)

    def backward_step(carry, block_id):
        r_index = (block_id // N_COL).astype(jnp.int32)
        c_index = (block_id % N_COL).astype(jnp.int32)
        live = (slot_ids < flat_count[block_id]).astype(jnp.float32)
        values = flat_values[block_id].astype(jnp.float32) * live[:, None, None]
        picked = grad_tiles[r_index * row_tiles + flat_rows[block_id]].astype(jnp.float32)
        products = jnp.einsum("kji,kjf->kif", values, picked)
        summed = jax.ops.segment_sum(products, flat_cols[block_id], num_segments=col_tiles)
        start = (c_index * col_tiles).astype(jnp.int32)
        current = lax.dynamic_slice_in_dim(carry, start, col_tiles, 0)
        carry = lax.dynamic_update_slice_in_dim(carry, current + rounded(summed), start, 0)
        return carry, None

    init_back = jnp.zeros((N_COL * col_tiles, TILE, F_IN), jnp.float32)
    back_all, _ = lax.scan(backward_step, init_back, jnp.arange(blocks, dtype=jnp.int32))
    grad_features = back_all.reshape(NODES, F_IN).astype(jnp.bfloat16)
    return hidden, grad_weight, grad_bias, grad_features
```

```python
import functools

import jax
import jax.numpy as jnp
from jax import lax
from jax.experimental import pallas as pl
from jax.experimental.pallas import tpu as pltpu
from jax.sharding import PartitionSpec as P

BF16 = jnp.bfloat16
F32 = jnp.float32
VMEM_LIMIT = 32 * 1024 * 1024
IN_VMEM = pl.BlockSpec(memory_space=pltpu.VMEM)
IN_ANY = pl.BlockSpec(memory_space=pl.ANY)
FIRST = 1 << 35
SOON = 3 << 28


def call(kernel, out_shape, in_specs, scratch=(), flops=0, nbytes=0, after=()):
    multi = isinstance(out_shape, (list, tuple))
    first, last = len(in_specs), len(in_specs) + len(after)

    def body(*refs):
        kernel(*refs[:first], *refs[last:])

    run = pl.pallas_call(
        body,
        out_shape=out_shape,
        in_specs=list(in_specs) + [IN_ANY] * len(after),
        out_specs=[IN_VMEM] * len(out_shape) if multi else IN_VMEM,
        scratch_shapes=list(scratch),
        compiler_params=pltpu.CompilerParams(vmem_limit_bytes=VMEM_LIMIT),
        cost_estimate=pl.CostEstimate(flops=flops, bytes_accessed=nbytes, transcendentals=0),
    )
    return lambda *args: run(*args, *after)


def lists_kernel(places, lists):
    slots, wide = places.shape[1], lists.shape[1]
    by_slot = jnp.broadcast_to(places[...].astype(F32), (slots, slots))
    down = by_slot.T[:, :1]
    slot = lax.broadcasted_iota(jnp.int32, (slots, wide), 0)
    at = lax.broadcasted_iota(jnp.int32, (slots, wide), 1)
    none = jnp.float32(slots)
    first = jnp.where(down == at.astype(F32), slot.astype(F32), none)
    lists[0:1, :] = jnp.min(first, axis=0, keepdims=True).astype(jnp.int32)
    later = slot[:, :slots] > at[:, :slots]
    follow = jnp.where((down == by_slot) & later, slot[:, :slots].astype(F32), none)
    lists[1:2, :slots] = jnp.min(follow, axis=0, keepdims=True).astype(jnp.int32)
    lists[1:2, slots:] = jnp.full((1, wide - slots), slots, jnp.int32)


def densify_kernel(lists, values, dense, head, after, many, list_sems):
    slots, tile, _ = values.shape
    row_tiles, col_tiles = dense.shape[0] // tile, dense.shape[1] // tile
    moves = [
        pltpu.make_async_copy(lists.at[pl.ds(0, 1)], head, list_sems.at[0]),
        pltpu.make_async_copy(lists.at[pl.ds(1, 1)], after, list_sems.at[1]),
    ]
    for copy in moves:
        copy.start()
    for copy in moves:
        copy.wait()

    def held(slot):
        return jnp.where(slot < slots, values[jnp.minimum(slot, slots - 1)], 0)

    def write(row, found):
        top = pl.ds(pl.multiple_of(row * tile, tile), tile)
        for col in range(col_tiles):
            place = row * col_tiles + col
            one = head[0, place]
            two = after[0, one]
            dense[top, col * tile : (col + 1) * tile] = held(one) + held(two)
            many[found] = place
            found += (after[0, two] < slots).astype(jnp.int32)
        return found

    found = lax.fori_loop(0, row_tiles, write, jnp.int32(0))

    def rewrite(at, carry):
        place = many[at]
        row = place // col_tiles
        top = pl.ds(pl.multiple_of(row * tile, tile), tile)
        left = pl.ds(pl.multiple_of((place - row * col_tiles) * tile, tile), tile)

        def more(state):
            slot, total = state
            return after[0, slot], total + values[slot].astype(F32)

        _, total = lax.while_loop(
            lambda state: state[0] < slots, more, (head[0, place], jnp.zeros((tile, tile), F32))
        )
        dense[top, left] = total.astype(BF16)
        return carry

    lax.fori_loop(0, found, rewrite, 0)


def forward_kernel(dense, own, y_1, near, y_near, far_4, y_4, far_6, out):
    pieces = (own, y_1, near, y_near, far_4, y_4, far_6)
    nodes = own.shape[0]
    r, c = lax.axis_index("row"), lax.axis_index("col")
    for at, j in enumerate((1, 3, 0, 2)):
        top = pl.ds(pl.multiple_of((c ^ j) * nodes, nodes), nodes)
        acc = jnp.zeros(own.shape, F32)
        for i, piece in enumerate(pieces):
            left = pl.ds(pl.multiple_of((r ^ i) * nodes, nodes), nodes)
            acc += jnp.dot(dense[top, left], piece[...], preferred_element_type=F32)
        out[at * nodes : (at + 1) * nodes, :] = acc


def finish_kernel(start, dense, most, y_6, out):
    nodes = y_6.shape[0]
    r, c = lax.axis_index("row"), lax.axis_index("col")
    left = pl.ds(pl.multiple_of((r ^ 7) * nodes, nodes), nodes)
    for at in range(2):
        j = (1, 3, 0, 2)[start + at]
        top = pl.ds(pl.multiple_of((c ^ j) * nodes, nodes), nodes)
        acc = most[(start + at) * nodes : (start + at + 1) * nodes, :]
        acc += jnp.dot(dense[top, left], y_6[...], preferred_element_type=F32)
        out[at * nodes : (at + 1) * nodes, :] = acc.astype(out.dtype)


def add_kernel(own, other, out):
    out[...] = (own[...] + other[...].astype(F32)).astype(out.dtype)


def layer_kernel(own, other, weight, bias, grad_out, grad_out_x, aggregate_out, grad_pre_out, hidden, grad_aggregate):
    nodes = hidden.shape[0]
    for at, grads in enumerate((grad_out, grad_out_x)):
        here = slice(at * nodes, (at + 1) * nodes)
        there = slice((1 - at) * nodes, (2 - at) * nodes)
        aggregate = (own[here, :].astype(F32) + other[there, :].astype(F32)).astype(BF16)
        aggregate_out[here, :] = aggregate
        preact = jnp.dot(aggregate, weight[...], preferred_element_type=F32) + bias[...]
        sig = jax.nn.sigmoid(preact)
        if at == 0:
            hidden[...] = (preact * sig).astype(BF16)
        slope = sig * (1.0 + preact * (1.0 - sig))
        grad_pre = (grads[...].astype(F32) * slope).astype(BF16)
        grad_pre_out[here, :] = grad_pre
        grad_aggregate[here, :] = lax.dot_general(
            grad_pre, weight[...], (((1,), (1,)), ((), ())), preferred_element_type=F32
        ).astype(BF16)


def pack(out, weights, bias):
    rows = weights.shape[0]
    high = bias.astype(BF16)
    low = (bias - high.astype(F32)).astype(BF16)
    at = lax.broadcasted_iota(jnp.int32, (out.shape[0] - rows, out.shape[1]), 0)
    out[:rows, :] = weights.astype(BF16)
    out[rows:, :] = jnp.where(at == 0, high.astype(F32), jnp.where(at == 1, low.astype(F32), 0.0)).astype(BF16)


def unpack(ref, rows):
    last = ref[rows:, :].astype(F32)
    return ref[:rows, :].astype(F32), last[0:1, :] + last[1:2, :]


def weight_kernel(aggregate, grad_pre, mine, theirs, full):
    core = lax.axis_index("col") & 1
    nodes = aggregate.shape[0] // 2
    first, second = slice(0, nodes), slice(nodes, 2 * nodes)
    by_node = (((0,), (0,)), ((), ()))
    full[...] = lax.dot_general(
        aggregate[first, :], grad_pre[first, :], by_node, preferred_element_type=F32
    ) + lax.dot_general(aggregate[second, :], grad_pre[second, :], by_node, preferred_element_type=F32)
    bias = jnp.sum(grad_pre[first, :].astype(F32), axis=0, keepdims=True) + jnp.sum(
        grad_pre[second, :].astype(F32), axis=0, keepdims=True
    )
    rows = full.shape[0] // 2
    for out, half in ((mine, core), (theirs, 1 - core)):
        pack(out, full[pl.ds(pl.multiple_of(half * rows, rows), rows), :], bias)


def merge_kernel(rows, own, other, out):
    weights, bias = unpack(own, rows)
    more_weights, more_bias = unpack(other, rows)
    pack(out, weights + more_weights, bias + more_bias)


def last_merge_kernel(own, near, half, bias):
    rows = half.shape[0]
    weights, biases = unpack(own, rows)
    more_weights, more_biases = unpack(near.at[near.shape[0] - own.shape[0] :], rows)
    half[...] = weights + more_weights
    bias[...] = biases + more_biases


def kept_kernel(places, dense, own, other, hidden_in, out, hidden):
    hidden[...] = hidden_in[...]
    backward_kernel(places, dense, own, other, out)


def backward_kernel(places, dense, own, other, out):
    nodes = own.shape[0] // 2
    r, c = lax.axis_index("row"), lax.axis_index("col")
    turned = [
        (j, ref[at * nodes : (at + 1) * nodes, :].T)
        for j, ref, at in ((0, own, 0), (2, own, 1), (1, other, 0), (3, other, 1))
    ]
    for at, i in enumerate(places):
        left = pl.ds(pl.multiple_of((r ^ i) * nodes, nodes), nodes)
        acc = jnp.zeros(out.shape[1:], F32)
        for j, piece in turned:
            top = pl.ds(pl.multiple_of((c ^ j) * nodes, nodes), nodes)
            acc += jnp.dot(piece, dense[top, left], preferred_element_type=F32)
        out[at] = acc.astype(out.dtype)


def far_kernel(kept, arrived, first, second):
    first[...] = (kept[0] + arrived[0].astype(F32)).astype(BF16)
    second[...] = (kept[1] + arrived[1].astype(F32)).astype(BF16)


def near_kernel(kept, arrived, part, near):
    rows = kept.shape[1]
    near[:rows, :] = (kept[3] + arrived[1].astype(F32)).astype(BF16)
    near[rows:, :] = part[...]


def gather_far_kernel(share_4, share_6, total):
    total[...] = share_4[...].astype(F32) + share_6[...].astype(F32)


def gather_near_kernel(arrived, near, gathered, total):
    total[...] = arrived[0].astype(F32) + near[: total.shape[0], :].astype(F32) + gathered[...]


def gather_own_kernel(kept, gathered, total):
    total[...] = kept[2] + gathered[...]


def last_kernel(gathered, mine, theirs, bias, grad_features, grad_weight, grad_bias):
    grad_features[...] = gathered[...].T.astype(BF16)
    grad_bias[...] = bias[...]
    core = lax.axis_index("col") & 1
    rows = mine.shape[0]
    for piece, half in ((mine, core), (theirs, 1 - core)):
        grad_weight[pl.ds(pl.multiple_of(half * rows, rows), rows), :] = piece[...]


def swap(value, axis, bits):
    size = lax.axis_size(axis)
    return lax.ppermute(value, axis, [(at, at ^ bits) for at in range(size)])


def dense_block(features, weight, bias, grad_out, tile_values, tile_rows, tile_cols, tile_count):
    n_row, n_col = lax.axis_size("row"), lax.axis_size("col")
    slots, tile = tile_values.shape[2:4]
    nodes, width_in = features.shape
    width_out = weight.shape[1]
    height, length = n_col * nodes, n_row * nodes
    positions = (height // tile) * (length // tile)
    whole = 2 * height * length * width_in
    shape = jax.ShapeDtypeStruct

    far = [swap(features, "row", 4), swap(features, "row", 6)]
    near = swap(features, "row", 2)
    grad_out_x = swap(grad_out, "col", 2)
    y_1, y_near = swap(features, "row", 1), swap(near, "row", 1)
    y_4, y_6 = swap(far[0], "row", 1), swap(far[1], "row", 1)
    places = jnp.where(
        jnp.arange(slots, dtype=jnp.int32) < tile_count[0, 0],
        tile_rows[0, 0] * (length // tile) + tile_cols[0, 0],
        positions,
    ).reshape(1, slots)
    wide = 128 * pl.cdiv(max(positions, slots + 1), 128)
    lists = call(lists_kernel, shape((2, wide), jnp.int32), [IN_VMEM], flops=FIRST)(places)
    dense = call(
        densify_kernel,
        shape((height, length), BF16),
        [IN_VMEM] * 2,
        [
            pltpu.SMEM((1, wide), jnp.int32),
            pltpu.SMEM((1, wide), jnp.int32),
            pltpu.SMEM((positions + 1,), jnp.int32),
            pltpu.SemaphoreType.DMA((2,)),
        ],
        nbytes=2 * tile_values.size * 2,
    )(lists, tile_values.reshape(slots, tile, tile))
    most = call(
        forward_kernel,
        shape((4 * nodes, width_in), F32),
        [IN_VMEM] * 8,
        flops=FIRST,
        nbytes=2 * height * length,
    )(dense, features, y_1, near, y_near, far[0], y_4, far[1])

    def finish(start, dtype):
        return call(
            functools.partial(finish_kernel, start),
            shape((2 * nodes, width_in), dtype),
            [IN_VMEM] * 3,
            flops=whole // 16,
            nbytes=height * length // 8,
        )(dense, most, y_6)

    core_share = swap(finish(0, BF16), "col", 1)
    half = call(
        add_kernel,
        shape((2 * nodes, width_in), BF16),
        [IN_VMEM] * 2,
        nbytes=16 * nodes * width_in,
        after=[grad_out_x],
    )(finish(2, F32), core_share)
    half_x = swap(half, "col", 2)
    aggregate, grad_pre, hidden, grad_aggregate = call(
        layer_kernel,
        [
            shape((2 * nodes, width_in), BF16),
            shape((2 * nodes, width_out), BF16),
            shape((nodes, width_out), BF16),
            shape((2 * nodes, width_in), BF16),
        ],
        [IN_VMEM] * 6,
        flops=8 * nodes * width_in * width_out,
        nbytes=16 * nodes * width_out,
    )(half, half_x, weight, bias.reshape(1, -1), grad_out, grad_out_x)
    grad_aggregate_core = swap(grad_aggregate, "col", 1)

    def backward(parts, dtype, after=()):
        return call(
            functools.partial(backward_kernel, parts),
            shape((len(parts), width_in, nodes), dtype),
            [IN_VMEM] * 3,
            flops=whole * len(parts) // n_row,
            nbytes=height * length * 2 * len(parts) // n_row,
            after=after,
        )(dense, grad_aggregate, grad_aggregate_core)

    sent_far = backward((5, 7), BF16)
    arrived_far = swap(sent_far, "row", 1)
    kept, hidden = call(
        functools.partial(kept_kernel, (4, 6, 0, 1)),
        [shape((4, width_in, nodes), F32), shape(hidden.shape, BF16)],
        [IN_VMEM] * 4,
        flops=whole // 2,
        nbytes=height * length,
        after=[sent_far],
    )(dense, grad_aggregate, grad_aggregate_core, hidden)
    turned = shape((width_in, nodes), BF16)
    share_4, share_6 = call(far_kernel, [turned] * 2, [IN_VMEM] * 2, nbytes=16 * nodes * width_in)(
        kept, arrived_far
    )

    mine, theirs = call(
        weight_kernel,
        [shape((width_in // 2 + 16, width_out), BF16)] * 2,
        [IN_VMEM] * 2,
        [pltpu.VMEM((width_in, width_out), F32)],
        flops=4 * nodes * width_in * width_out,
        nbytes=8 * width_in * width_out,
    )(aggregate, grad_pre)

    def merge(own, other, after=()):
        return call(
            functools.partial(merge_kernel, width_in // 2),
            shape(own.shape, BF16),
            [IN_VMEM] * 2,
            nbytes=6 * own.size,
            after=after,
        )(own, other)

    part = merge(mine, swap(theirs, "col", 1), [sent_far])
    part = merge(part, swap(part, "row", 2))
    sent_near = backward((2, 3), BF16, [part])
    arrived_near = swap(sent_near, "row", 2)
    part = merge(part, swap(part, "row", 4))
    near = call(
        near_kernel,
        shape((width_in + part.shape[0], nodes), BF16),
        [IN_VMEM] * 3,
        nbytes=8 * nodes * width_in,
    )(kept, arrived_near, part)
    near = swap(near, "row", 1)
    half_weight, bias_sum = call(
        last_merge_kernel,
        [shape((width_in // 2, width_out), F32), shape((1, width_out), F32)],
        [IN_VMEM] * 2,
        nbytes=8 * part.size,
    )(part, near)
    turned = shape((width_in, nodes), F32)
    gathered = call(gather_far_kernel, turned, [IN_VMEM] * 2, flops=SOON)(
        swap(share_4, "row", 4), swap(share_6, "row", 6)
    )
    gathered = call(gather_near_kernel, turned, [IN_VMEM] * 3)(arrived_near, near, gathered)
    gathered = call(gather_own_kernel, turned, [IN_VMEM] * 2, flops=FIRST)(kept, gathered)
    grad_features, grad_weight, grad_bias = call(
        last_kernel,
        [
            shape((nodes, width_in), BF16),
            shape((width_in, width_out), F32),
            shape((1, width_out), F32),
        ],
        [IN_VMEM] * 4,
        nbytes=16 * nodes * width_in,
    )(gathered, half_weight, swap(half_weight, "col", 1), bias_sum)
    return hidden, grad_weight, grad_bias.reshape(-1), grad_features


def sparse_block(features, weight, bias, grad_out, tile_values, tile_rows, tile_cols, tile_count):
    values = tile_values[0, 0]
    slot_rows = tile_rows[0, 0]
    slot_cols = tile_cols[0, 0]
    tile_size = values.shape[1]
    width_in = features.shape[1]
    node_rows = features.shape[0]
    live = (jnp.arange(values.shape[0]) < tile_count[0, 0]).astype(values.dtype)
    values = values * live[:, None, None]
    panel = lax.all_gather(features, "row", axis=0, tiled=True)
    panel_tiles = panel.reshape(-1, tile_size, width_in)
    picked = panel_tiles[slot_cols]
    products = jnp.einsum("kij,kjf->kif", values, picked, preferred_element_type=F32)
    row_segments = lax.axis_size("col") * node_rows // tile_size
    partial_value = jax.ops.segment_sum(products, slot_rows, num_segments=row_segments).reshape(
        -1, width_in
    )
    aggregate = lax.psum_scatter(
        partial_value.astype(BF16), "col", scatter_dimension=0, tiled=True
    )
    preact = jnp.dot(aggregate, weight, preferred_element_type=F32) + bias
    sigmoid_pre = jax.nn.sigmoid(preact)
    hidden = (preact * sigmoid_pre).astype(BF16)
    slope_factor = sigmoid_pre * (1.0 + preact * (1.0 - sigmoid_pre))
    grad_pre = (grad_out.astype(F32) * slope_factor).astype(BF16)
    local_weight = jnp.dot(aggregate.T, grad_pre, preferred_element_type=F32)
    local_bias = jnp.sum(grad_pre.astype(F32), axis=0)
    grad_weight, grad_bias = lax.psum((local_weight, local_bias), ("row", "col"))
    grad_aggregate = jnp.dot(grad_pre, weight.T, preferred_element_type=F32).astype(BF16)
    block_aggregate = lax.all_gather(grad_aggregate, "col", axis=0, tiled=True)
    block_tiles = block_aggregate.reshape(-1, tile_size, width_in)
    picked_back = block_tiles[slot_rows]
    back_products = jnp.einsum(
        "kji,kjf->kif", values, picked_back, preferred_element_type=F32
    )
    col_segments = lax.axis_size("row") * node_rows // tile_size
    partial_back = jax.ops.segment_sum(back_products, slot_cols, num_segments=col_segments).reshape(
        -1, width_in
    )
    grad_features = lax.psum_scatter(
        partial_back.astype(BF16), "row", scatter_dimension=0, tiled=True
    )
    return hidden, grad_weight, grad_bias, grad_features


def per_device(features, weight, bias, grad_out, tile_values, tile_rows, tile_cols, tile_count):
    n_row, n_col = lax.axis_size("row"), lax.axis_size("col")
    slots, tile = tile_values.shape[2:4]
    nodes = features.shape[0]
    positions = n_row * n_col * (nodes // tile) ** 2
    block = dense_block if (n_row, n_col) == (8, 4) and positions <= 2 * slots else sparse_block
    return block(features, weight, bias, grad_out, tile_values, tile_rows, tile_cols, tile_count)


def solution(mesh):
    return jax.shard_map(
        per_device,
        mesh=mesh,
        in_specs=(
            P(("col", "row"), None),
            P(),
            P(),
            P(("row", "col"), None),
            P("row", "col", None, None, None),
            P("row", "col", None),
            P("row", "col", None),
            P("row", "col"),
        ),
        out_specs=(P(("row", "col"), None), P(), P(), P(("col", "row"), None)),
        check_vma=False,
    )
```

```python
import functools

import jax
import jax.numpy as jnp
from jax import lax
from jax.experimental import pallas as pl
from jax.experimental.pallas import tpu as pltpu
from jax.sharding import PartitionSpec as P

BF16 = jnp.bfloat16
F32 = jnp.float32
VMEM_LIMIT = 32 * 1024 * 1024
IN_VMEM = pl.BlockSpec(memory_space=pltpu.VMEM)
IN_ANY = pl.BlockSpec(memory_space=pl.ANY)
FIRST = 1 << 35
SOON = 3 << 28


def call(kernel, out_shape, in_specs, scratch=(), flops=0, nbytes=0, after=()):
    multi = isinstance(out_shape, (list, tuple))
    first, last = len(in_specs), len(in_specs) + len(after)

    def body(*refs):
        kernel(*refs[:first], *refs[last:])

    run = pl.pallas_call(
        body,
        out_shape=out_shape,
        in_specs=list(in_specs) + [IN_ANY] * len(after),
        out_specs=[IN_VMEM] * len(out_shape) if multi else IN_VMEM,
        scratch_shapes=list(scratch),
        compiler_params=pltpu.CompilerParams(vmem_limit_bytes=VMEM_LIMIT),
        cost_estimate=pl.CostEstimate(flops=flops, bytes_accessed=nbytes, transcendentals=0),
    )
    return lambda *args: run(*args, *after)


def relay_kernel(source, target):
    target[...] = source[...]


def lists_kernel(col_tiles, rows, cols, lists):
    slots, wide = rows.shape[2], lists.shape[1]
    by_slot = jnp.broadcast_to((rows[0] * col_tiles + cols[0]).astype(F32), (slots, slots))
    down = by_slot.T[:, :1]
    slot = lax.broadcasted_iota(jnp.int32, (slots, wide), 0)
    at = lax.broadcasted_iota(jnp.int32, (slots, wide), 1)
    none = jnp.float32(slots)
    first = jnp.where(down == at.astype(F32), slot.astype(F32), none)
    lists[0:1, :] = jnp.min(first, axis=0, keepdims=True).astype(jnp.int32)
    later = slot[:, :slots] > at[:, :slots]
    follow = jnp.where((down == by_slot) & later, slot[:, :slots].astype(F32), none)
    lists[1:2, :slots] = jnp.min(follow, axis=0, keepdims=True).astype(jnp.int32)
    lists[1:2, slots:] = jnp.full((1, wide - slots), slots, jnp.int32)


def densify_kernel(lists, count, values, dense, head, after, many, sems):
    slots, tile, _ = values.shape
    row_tiles, col_tiles = dense.shape[0] // tile, dense.shape[1] // tile
    moves = [
        pltpu.make_async_copy(lists.at[pl.ds(0, 1)], head, sems.at[0]),
        pltpu.make_async_copy(lists.at[pl.ds(1, 1)], after, sems.at[1]),
    ]
    for copy in moves:
        copy.start()
    for copy in moves:
        copy.wait()
    end = count[0, 0]

    def held(slot):
        return jnp.where(slot < end, values[jnp.minimum(slot, slots - 1)], 0)

    def write(row, found):
        top = pl.ds(pl.multiple_of(row * tile, tile), tile)
        for col in range(col_tiles):
            place = row * col_tiles + col
            one = head[0, place]
            two = after[0, one]
            dense[top, col * tile : (col + 1) * tile] = held(one) + held(two)
            many[found] = place
            found += (after[0, two] < end).astype(jnp.int32)
        return found

    found = lax.fori_loop(0, row_tiles, write, jnp.int32(0))

    def rewrite(at, carry):
        place = many[at]
        row = place // col_tiles
        top = pl.ds(pl.multiple_of(row * tile, tile), tile)
        left = pl.ds(pl.multiple_of((place - row * col_tiles) * tile, tile), tile)

        def more(state):
            slot, total = state
            return after[0, slot], total + values[slot].astype(F32)

        one = head[0, place]
        two = after[0, one]
        three = after[0, two]
        total = values[one].astype(F32) + values[two].astype(F32) + values[three].astype(F32)
        _, total = lax.while_loop(lambda state: state[0] < end, more, (after[0, three], total))
        dense[top, left] = total.astype(BF16)
        return carry

    lax.fori_loop(0, found, rewrite, 0)


def forward_kernel(places, dense, *refs):
    pieces, out = refs[:-1], refs[-1]
    nodes = pieces[0].shape[0]
    r, c = lax.axis_index("row"), lax.axis_index("col")
    for at, j in enumerate(places):
        top = pl.ds(pl.multiple_of((c ^ j) * nodes, nodes), nodes)
        acc = jnp.zeros(pieces[0].shape, F32)
        for i, piece in enumerate(pieces):
            left = pl.ds(pl.multiple_of((r ^ i) * nodes, nodes), nodes)
            acc += jnp.dot(dense[top, left], piece[...], preferred_element_type=F32)
        out[at * nodes : (at + 1) * nodes, :] = acc.astype(out.dtype)


def add_kernel(own, other, out):
    out[...] = (own[...] + other[...].astype(F32)).astype(out.dtype)


def layer_kernel(own, other, weight, bias, grad_out, grad_out_x, aggregate_out, grad_pre_out, hidden, grad_aggregate):
    nodes = hidden.shape[0]
    for at, grads in enumerate((grad_out, grad_out_x)):
        here = slice(at * nodes, (at + 1) * nodes)
        there = slice((1 - at) * nodes, (2 - at) * nodes)
        aggregate = (own[here, :].astype(F32) + other[there, :].astype(F32)).astype(BF16)
        aggregate_out[here, :] = aggregate
        preact = jnp.dot(aggregate, weight[...], preferred_element_type=F32) + bias[...]
        sig = jax.nn.sigmoid(preact)
        if at == 0:
            hidden[...] = (preact * sig).astype(BF16)
        slope = sig * (1.0 + preact * (1.0 - sig))
        grad_pre = (grads[...].astype(F32) * slope).astype(BF16)
        grad_pre_out[here, :] = grad_pre
        grad_aggregate[here, :] = lax.dot_general(
            grad_pre, weight[...], (((1,), (1,)), ((), ())), preferred_element_type=F32
        ).astype(BF16)


def pack(out, weights, bias):
    rows = weights.shape[0]
    high = bias.astype(BF16)
    low = (bias - high.astype(F32)).astype(BF16)
    at = lax.broadcasted_iota(jnp.int32, (out.shape[0] - rows, out.shape[1]), 0)
    out[:rows, :] = weights.astype(BF16)
    out[rows:, :] = jnp.where(at == 0, high.astype(F32), jnp.where(at == 1, low.astype(F32), 0.0)).astype(BF16)


def unpack(ref, rows):
    last = ref[rows:, :].astype(F32)
    return ref[:rows, :].astype(F32), last[0:1, :] + last[1:2, :]


def weight_kernel(aggregate, grad_pre, mine, theirs, full):
    core = lax.axis_index("col") & 1
    nodes = aggregate.shape[0] // 2
    first, second = slice(0, nodes), slice(nodes, 2 * nodes)
    by_node = (((0,), (0,)), ((), ()))
    full[...] = lax.dot_general(
        aggregate[first, :], grad_pre[first, :], by_node, preferred_element_type=F32
    ) + lax.dot_general(aggregate[second, :], grad_pre[second, :], by_node, preferred_element_type=F32)
    bias = jnp.sum(grad_pre[first, :].astype(F32), axis=0, keepdims=True) + jnp.sum(
        grad_pre[second, :].astype(F32), axis=0, keepdims=True
    )
    rows = full.shape[0] // 2
    for out, half in ((mine, core), (theirs, 1 - core)):
        pack(out, full[pl.ds(pl.multiple_of(half * rows, rows), rows), :], bias)


def merge_kernel(rows, own, other, out):
    weights, bias = unpack(own, rows)
    more_weights, more_bias = unpack(other, rows)
    pack(out, weights + more_weights, bias + more_bias)


def last_merge_kernel(own, near, half, bias):
    rows = half.shape[0]
    weights, biases = unpack(own, rows)
    more_weights, more_biases = unpack(near.at[near.shape[0] - own.shape[0] :], rows)
    half[...] = weights + more_weights
    bias[...] = biases + more_biases


def kept_kernel(places, dense, own, other, hidden_in, out, hidden):
    hidden[...] = hidden_in[...]
    backward_kernel(places, dense, own, other, out)


def backward_kernel(places, dense, own, other, out):
    nodes = own.shape[0] // 2
    r, c = lax.axis_index("row"), lax.axis_index("col")
    turned = [
        (j, ref[at * nodes : (at + 1) * nodes, :].T)
        for j, ref, at in ((0, own, 0), (2, own, 1), (1, other, 0), (3, other, 1))
    ]
    for at, i in enumerate(places):
        left = pl.ds(pl.multiple_of((r ^ i) * nodes, nodes), nodes)
        acc = jnp.zeros(out.shape[1:], F32)
        for j, piece in turned:
            top = pl.ds(pl.multiple_of((c ^ j) * nodes, nodes), nodes)
            acc += jnp.dot(piece, dense[top, left], preferred_element_type=F32)
        out[at] = acc.astype(out.dtype)


def far_kernel(kept, arrived, first, second):
    first[...] = (kept[0] + arrived[0].astype(F32)).astype(BF16)
    second[...] = (kept[1] + arrived[1].astype(F32)).astype(BF16)


def near_kernel(kept, arrived, part, near):
    rows = kept.shape[1]
    near[:rows, :] = (kept[3] + arrived[1].astype(F32)).astype(BF16)
    near[rows:, :] = part[...]


def gather_far_kernel(share_4, share_6, total):
    total[...] = share_4[...].astype(F32) + share_6[...].astype(F32)


def gather_near_kernel(arrived, near, gathered, total):
    total[...] = arrived[0].astype(F32) + near[: total.shape[0], :].astype(F32) + gathered[...]


def gather_own_kernel(kept, gathered, total):
    total[...] = kept[2] + gathered[...]


def last_kernel(gathered, mine, theirs, bias, grad_features, grad_weight, grad_bias):
    grad_features[...] = gathered[...].T.astype(BF16)
    grad_bias[...] = bias[...]
    core = lax.axis_index("col") & 1
    rows = mine.shape[0]
    for piece, half in ((mine, core), (theirs, 1 - core)):
        grad_weight[pl.ds(pl.multiple_of(half * rows, rows), rows), :] = piece[...]


def swap(value, axis, bits):
    size = lax.axis_size(axis)
    return lax.ppermute(value, axis, [(at, at ^ bits) for at in range(size)])


def dense_block(features, weight, bias, grad_out, tile_values, tile_rows, tile_cols, tile_count):
    n_row, n_col = lax.axis_size("row"), lax.axis_size("col")
    slots, tile = tile_values.shape[2:4]
    nodes, width_in = features.shape
    width_out = weight.shape[1]
    height, length = n_col * nodes, n_row * nodes
    positions = (height // tile) * (length // tile)
    whole = 2 * height * length * width_in
    shape = jax.ShapeDtypeStruct

    far = [swap(features, "row", 4), swap(features, "row", 6)]
    near = call(relay_kernel, shape(features.shape, BF16), [IN_VMEM], flops=FIRST)(swap(features, "row", 2))
    grad_out_x = swap(grad_out, "col", 2)
    y_1, y_near = swap(features, "row", 1), swap(near, "row", 1)
    y_4, y_6 = swap(far[0], "row", 1), swap(far[1], "row", 1)
    wide = 128 * pl.cdiv(max(positions, slots + 1), 128)
    lists = call(
        functools.partial(lists_kernel, length // tile), shape((2, wide), jnp.int32), [IN_VMEM] * 2
    )(tile_rows, tile_cols)
    dense = call(
        densify_kernel,
        shape((height, length), BF16),
        [IN_VMEM, pl.BlockSpec(memory_space=pltpu.SMEM), IN_VMEM],
        [
            pltpu.SMEM((1, wide), jnp.int32),
            pltpu.SMEM((1, wide), jnp.int32),
            pltpu.SMEM((positions + 1,), jnp.int32),
            pltpu.SemaphoreType.DMA((2,)),
        ],
        nbytes=2 * tile_values.size * 2,
    )(lists, tile_count, tile_values.reshape(slots, tile, tile))
    def forward(parts, dtype):
        return call(
            functools.partial(forward_kernel, parts),
            shape((2 * nodes, width_in), dtype),
            [IN_VMEM] * (1 + n_row),
            flops=whole // 2,
            nbytes=height * length,
        )(dense, features, y_1, near, y_near, far[0], y_4, far[1], y_6)

    core_share = swap(forward((1, 3), BF16), "col", 1)
    half = call(
        add_kernel,
        shape((2 * nodes, width_in), BF16),
        [IN_VMEM] * 2,
        nbytes=16 * nodes * width_in,
        after=[grad_out_x],
    )(forward((0, 2), F32), core_share)
    half_x = swap(half, "col", 2)
    aggregate, grad_pre, hidden, grad_aggregate = call(
        layer_kernel,
        [
            shape((2 * nodes, width_in), BF16),
            shape((2 * nodes, width_out), BF16),
            shape((nodes, width_out), BF16),
            shape((2 * nodes, width_in), BF16),
        ],
        [IN_VMEM] * 6,
        flops=8 * nodes * width_in * width_out,
        nbytes=16 * nodes * width_out,
    )(half, half_x, weight, bias.reshape(1, -1), grad_out, grad_out_x)
    grad_aggregate_core = swap(grad_aggregate, "col", 1)

    def backward(parts, dtype, after=()):
        return call(
            functools.partial(backward_kernel, parts),
            shape((len(parts), width_in, nodes), dtype),
            [IN_VMEM] * 3,
            flops=whole * len(parts) // n_row,
            nbytes=height * length * 2 * len(parts) // n_row,
            after=after,
        )(dense, grad_aggregate, grad_aggregate_core)

    sent_far = backward((5, 7), BF16)
    arrived_far = swap(sent_far, "row", 1)
    kept, hidden = call(
        functools.partial(kept_kernel, (4, 6, 0, 1)),
        [shape((4, width_in, nodes), F32), shape(hidden.shape, BF16)],
        [IN_VMEM] * 4,
        flops=whole // 2,
        nbytes=height * length,
        after=[sent_far],
    )(dense, grad_aggregate, grad_aggregate_core, hidden)
    turned = shape((width_in, nodes), BF16)
    share_4, share_6 = call(far_kernel, [turned] * 2, [IN_VMEM] * 2, nbytes=16 * nodes * width_in)(
        kept, arrived_far
    )

    mine, theirs = call(
        weight_kernel,
        [shape((width_in // 2 + 16, width_out), BF16)] * 2,
        [IN_VMEM] * 2,
        [pltpu.VMEM((width_in, width_out), F32)],
        flops=4 * nodes * width_in * width_out,
        nbytes=8 * width_in * width_out,
    )(aggregate, grad_pre)

    def merge(own, other, after=()):
        return call(
            functools.partial(merge_kernel, width_in // 2),
            shape(own.shape, BF16),
            [IN_VMEM] * 2,
            nbytes=6 * own.size,
            after=after,
        )(own, other)

    part = merge(mine, swap(theirs, "col", 1), [sent_far])
    part = merge(part, swap(part, "row", 2), [kept])
    sent_near = backward((2, 3), BF16, [part])
    arrived_near = swap(sent_near, "row", 2)
    part = merge(part, swap(part, "row", 4))
    near = call(
        near_kernel,
        shape((width_in + part.shape[0], nodes), BF16),
        [IN_VMEM] * 3,
        nbytes=8 * nodes * width_in,
    )(kept, arrived_near, part)
    near = swap(near, "row", 1)
    half_weight, bias_sum = call(
        last_merge_kernel,
        [shape((width_in // 2, width_out), F32), shape((1, width_out), F32)],
        [IN_VMEM] * 2,
        nbytes=8 * part.size,
    )(part, near)
    turned = shape((width_in, nodes), F32)
    gathered = call(gather_far_kernel, turned, [IN_VMEM] * 2, flops=SOON)(
        swap(share_4, "row", 4), swap(share_6, "row", 6)
    )
    gathered = call(gather_near_kernel, turned, [IN_VMEM] * 3)(arrived_near, near, gathered)
    gathered = call(gather_own_kernel, turned, [IN_VMEM] * 2, flops=FIRST)(kept, gathered)
    grad_features, grad_weight, grad_bias = call(
        last_kernel,
        [
            shape((nodes, width_in), BF16),
            shape((width_in, width_out), F32),
            shape((1, width_out), F32),
        ],
        [IN_VMEM] * 4,
        nbytes=16 * nodes * width_in,
    )(gathered, half_weight, swap(half_weight, "col", 1), bias_sum)
    return hidden, grad_weight, grad_bias.reshape(-1), grad_features


def sparse_block(features, weight, bias, grad_out, tile_values, tile_rows, tile_cols, tile_count):
    values = tile_values[0, 0]
    slot_rows = tile_rows[0, 0]
    slot_cols = tile_cols[0, 0]
    tile_size = values.shape[1]
    width_in = features.shape[1]
    node_rows = features.shape[0]
    live = (jnp.arange(values.shape[0]) < tile_count[0, 0]).astype(values.dtype)
    values = values * live[:, None, None]
    panel = lax.all_gather(features, "row", axis=0, tiled=True)
    panel_tiles = panel.reshape(-1, tile_size, width_in)
    picked = panel_tiles[slot_cols]
    products = jnp.einsum("kij,kjf->kif", values, picked, preferred_element_type=F32)
    row_segments = lax.axis_size("col") * node_rows // tile_size
    partial_value = jax.ops.segment_sum(products, slot_rows, num_segments=row_segments).reshape(
        -1, width_in
    )
    aggregate = lax.psum_scatter(
        partial_value.astype(BF16), "col", scatter_dimension=0, tiled=True
    )
    preact = jnp.dot(aggregate, weight, preferred_element_type=F32) + bias
    sigmoid_pre = jax.nn.sigmoid(preact)
    hidden = (preact * sigmoid_pre).astype(BF16)
    slope_factor = sigmoid_pre * (1.0 + preact * (1.0 - sigmoid_pre))
    grad_pre = (grad_out.astype(F32) * slope_factor).astype(BF16)
    local_weight = jnp.dot(aggregate.T, grad_pre, preferred_element_type=F32)
    local_bias = jnp.sum(grad_pre.astype(F32), axis=0)
    grad_weight, grad_bias = lax.psum((local_weight, local_bias), ("row", "col"))
    grad_aggregate = jnp.dot(grad_pre, weight.T, preferred_element_type=F32).astype(BF16)
    block_aggregate = lax.all_gather(grad_aggregate, "col", axis=0, tiled=True)
    block_tiles = block_aggregate.reshape(-1, tile_size, width_in)
    picked_back = block_tiles[slot_rows]
    back_products = jnp.einsum(
        "kji,kjf->kif", values, picked_back, preferred_element_type=F32
    )
    col_segments = lax.axis_size("row") * node_rows // tile_size
    partial_back = jax.ops.segment_sum(back_products, slot_cols, num_segments=col_segments).reshape(
        -1, width_in
    )
    grad_features = lax.psum_scatter(
        partial_back.astype(BF16), "row", scatter_dimension=0, tiled=True
    )
    return hidden, grad_weight, grad_bias, grad_features


def per_device(features, weight, bias, grad_out, tile_values, tile_rows, tile_cols, tile_count):
    n_row, n_col = lax.axis_size("row"), lax.axis_size("col")
    slots, tile = tile_values.shape[2:4]
    nodes = features.shape[0]
    positions = n_row * n_col * (nodes // tile) ** 2
    block = dense_block if (n_row, n_col) == (8, 4) and positions <= 2 * slots else sparse_block
    return block(features, weight, bias, grad_out, tile_values, tile_rows, tile_cols, tile_count)


def solution(mesh):
    return jax.shard_map(
        per_device,
        mesh=mesh,
        in_specs=(
            P(("col", "row"), None),
            P(),
            P(),
            P(("row", "col"), None),
            P("row", "col", None, None, None),
            P("row", "col", None),
            P("row", "col", None),
            P("row", "col"),
        ),
        out_specs=(P(("row", "col"), None), P(), P(), P(("col", "row"), None)),
        check_vma=False,
    )
```

```python
import functools

import jax
import jax.numpy as jnp
from jax import lax
from jax.experimental import pallas as pl
from jax.experimental.pallas import tpu as pltpu
from jax.sharding import PartitionSpec as P

BF16 = jnp.bfloat16
F32 = jnp.float32
VMEM_LIMIT = 32 * 1024 * 1024
IN_VMEM = pl.BlockSpec(memory_space=pltpu.VMEM)
IN_SMEM = pl.BlockSpec(memory_space=pltpu.SMEM)
IN_ANY = pl.BlockSpec(memory_space=pl.ANY)
FIRST = 1 << 35
SOON = 3 << 28


def call(kernel, out_shape, in_specs, scratch=(), flops=0, nbytes=0, after=()):
    multi = isinstance(out_shape, (list, tuple))
    first, last = len(in_specs), len(in_specs) + len(after)

    def body(*refs):
        kernel(*refs[:first], *refs[last:])

    run = pl.pallas_call(
        body,
        out_shape=out_shape,
        in_specs=list(in_specs) + [IN_ANY] * len(after),
        out_specs=[IN_VMEM] * len(out_shape) if multi else IN_VMEM,
        scratch_shapes=list(scratch),
        compiler_params=pltpu.CompilerParams(vmem_limit_bytes=VMEM_LIMIT),
        cost_estimate=pl.CostEstimate(flops=flops, bytes_accessed=nbytes, transcendentals=0),
    )
    return lambda *args: run(*args, *after)


def relay_kernel(source, target):
    target[...] = source[...]


def lists_kernel(col_tiles, rows, cols, count, lists):
    slots, wide = rows.shape[2], lists.shape[1]
    live = lax.broadcasted_iota(jnp.int32, (1, slots), 1) < count[0, 0]
    places = jnp.where(live, rows[0] * col_tiles + cols[0], wide)
    by_slot = jnp.broadcast_to(places.astype(F32), (slots, slots))
    down = by_slot.T[:, :1]
    slot = lax.broadcasted_iota(jnp.int32, (slots, wide), 0)
    at = lax.broadcasted_iota(jnp.int32, (slots, wide), 1)
    none = jnp.float32(slots)
    first = jnp.where(down == at.astype(F32), slot.astype(F32), none)
    lists[0:1, :] = jnp.min(first, axis=0, keepdims=True).astype(jnp.int32)
    later = slot[:, :slots] > at[:, :slots]
    follow = jnp.where((down == by_slot) & later, slot[:, :slots].astype(F32), none)
    lists[1:2, :slots] = jnp.min(follow, axis=0, keepdims=True).astype(jnp.int32)
    lists[1:2, slots:] = jnp.full((1, wide - slots), slots, jnp.int32)


def densify_kernel(lists, values, dense, head, after, many, sems):
    slots, tile, _ = values.shape
    row_tiles, col_tiles = dense.shape[0] // tile, dense.shape[1] // tile
    moves = [
        pltpu.make_async_copy(lists.at[pl.ds(0, 1)], head, sems.at[0]),
        pltpu.make_async_copy(lists.at[pl.ds(1, 1)], after, sems.at[1]),
    ]
    for copy in moves:
        copy.start()
    for copy in moves:
        copy.wait()

    def held(slot):
        return jnp.where(slot < slots, values[jnp.minimum(slot, slots - 1)], 0)

    def write(row, found):
        top = pl.ds(pl.multiple_of(row * tile, tile), tile)
        for col in range(col_tiles):
            place = row * col_tiles + col
            one = head[0, place]
            two = after[0, one]
            dense[top, col * tile : (col + 1) * tile] = held(one) + held(two)
            many[found] = place
            found += (after[0, two] < slots).astype(jnp.int32)
        return found

    found = lax.fori_loop(0, row_tiles, write, jnp.int32(0))

    def rewrite(at, carry):
        place = many[at]
        row = place // col_tiles
        top = pl.ds(pl.multiple_of(row * tile, tile), tile)
        left = pl.ds(pl.multiple_of((place - row * col_tiles) * tile, tile), tile)

        def more(state):
            slot, total = state
            return after[0, slot], total + values[slot].astype(F32)

        one = head[0, place]
        two = after[0, one]
        three = after[0, two]
        total = values[one].astype(F32) + values[two].astype(F32) + values[three].astype(F32)
        _, total = lax.while_loop(lambda state: state[0] < slots, more, (after[0, three], total))
        dense[top, left] = total.astype(BF16)
        return carry

    lax.fori_loop(0, found, rewrite, 0)


def forward_kernel(places, dense, *refs):
    pieces, out = refs[:-1], refs[-1]
    nodes = pieces[0].shape[0]
    r, c = lax.axis_index("row"), lax.axis_index("col")
    for at, j in enumerate(places):
        top = pl.ds(pl.multiple_of((c ^ j) * nodes, nodes), nodes)
        acc = jnp.zeros(pieces[0].shape, F32)
        for i, piece in enumerate(pieces):
            left = pl.ds(pl.multiple_of((r ^ i) * nodes, nodes), nodes)
            acc += jnp.dot(dense[top, left], piece[...], preferred_element_type=F32)
        out[at * nodes : (at + 1) * nodes, :] = acc.astype(out.dtype)


def add_kernel(own, other, out):
    out[...] = (own[...] + other[...].astype(F32)).astype(out.dtype)


def layer_kernel(own, other, weight, bias, grad_out, grad_out_x, aggregate_out, grad_pre_out, hidden, grad_aggregate):
    nodes = hidden.shape[0]
    for at, grads in enumerate((grad_out, grad_out_x)):
        here = slice(at * nodes, (at + 1) * nodes)
        there = slice((1 - at) * nodes, (2 - at) * nodes)
        aggregate = (own[here, :].astype(F32) + other[there, :].astype(F32)).astype(BF16)
        aggregate_out[here, :] = aggregate
        preact = jnp.dot(aggregate, weight[...], preferred_element_type=F32) + bias[...]
        sig = jax.nn.sigmoid(preact)
        if at == 0:
            hidden[...] = (preact * sig).astype(BF16)
        slope = sig * (1.0 + preact * (1.0 - sig))
        grad_pre = (grads[...].astype(F32) * slope).astype(BF16)
        grad_pre_out[here, :] = grad_pre
        grad_aggregate[here, :] = lax.dot_general(
            grad_pre, weight[...], (((1,), (1,)), ((), ())), preferred_element_type=F32
        ).astype(BF16)


def pack(out, weights, bias):
    rows = weights.shape[0]
    high = bias.astype(BF16)
    low = (bias - high.astype(F32)).astype(BF16)
    at = lax.broadcasted_iota(jnp.int32, (out.shape[0] - rows, out.shape[1]), 0)
    out[:rows, :] = weights.astype(BF16)
    out[rows:, :] = jnp.where(at == 0, high.astype(F32), jnp.where(at == 1, low.astype(F32), 0.0)).astype(BF16)


def unpack(ref, rows):
    last = ref[rows:, :].astype(F32)
    return ref[:rows, :].astype(F32), last[0:1, :] + last[1:2, :]


def weight_kernel(aggregate, grad_pre, mine, theirs, full):
    core = lax.axis_index("col") & 1
    nodes = aggregate.shape[0] // 2
    first, second = slice(0, nodes), slice(nodes, 2 * nodes)
    by_node = (((0,), (0,)), ((), ()))
    full[...] = lax.dot_general(
        aggregate[first, :], grad_pre[first, :], by_node, preferred_element_type=F32
    ) + lax.dot_general(aggregate[second, :], grad_pre[second, :], by_node, preferred_element_type=F32)
    bias = jnp.sum(grad_pre[first, :].astype(F32), axis=0, keepdims=True) + jnp.sum(
        grad_pre[second, :].astype(F32), axis=0, keepdims=True
    )
    rows = full.shape[0] // 2
    for out, half in ((mine, core), (theirs, 1 - core)):
        pack(out, full[pl.ds(pl.multiple_of(half * rows, rows), rows), :], bias)


def merge_kernel(rows, own, other, out):
    weights, bias = unpack(own, rows)
    more_weights, more_bias = unpack(other, rows)
    pack(out, weights + more_weights, bias + more_bias)


def last_merge_kernel(own, near, half, bias):
    rows = half.shape[0]
    weights, biases = unpack(own, rows)
    more_weights, more_biases = unpack(near.at[near.shape[0] - own.shape[0] :], rows)
    half[...] = weights + more_weights
    bias[...] = biases + more_biases


def kept_kernel(places, dense, own, other, hidden_in, out, hidden):
    hidden[...] = hidden_in[...]
    backward_kernel(places, dense, own, other, out)


def backward_kernel(places, dense, own, other, out):
    nodes = own.shape[0] // 2
    r, c = lax.axis_index("row"), lax.axis_index("col")
    turned = [
        (j, ref[at * nodes : (at + 1) * nodes, :].T)
        for j, ref, at in ((0, own, 0), (2, own, 1), (1, other, 0), (3, other, 1))
    ]
    for at, i in enumerate(places):
        left = pl.ds(pl.multiple_of((r ^ i) * nodes, nodes), nodes)
        acc = jnp.zeros(out.shape[1:], F32)
        for j, piece in turned:
            top = pl.ds(pl.multiple_of((c ^ j) * nodes, nodes), nodes)
            acc += jnp.dot(piece, dense[top, left], preferred_element_type=F32)
        out[at] = acc.astype(out.dtype)


def far_kernel(kept, arrived, first, second):
    first[...] = (kept[0] + arrived[0].astype(F32)).astype(BF16)
    second[...] = (kept[1] + arrived[1].astype(F32)).astype(BF16)


def near_kernel(kept, arrived, part, near):
    rows = kept.shape[1]
    near[:rows, :] = (kept[3] + arrived[1].astype(F32)).astype(BF16)
    near[rows:, :] = part[...]


def gather_far_kernel(kept, share_4, total):
    total[...] = kept[2] + share_4[...].astype(F32)


def gather_near_kernel(arrived, near, gathered, total):
    total[...] = arrived[0].astype(F32) + near[: total.shape[0], :].astype(F32) + gathered[...]


def gather_last_kernel(share_6, gathered, total):
    total[...] = share_6[...].astype(F32) + gathered[...]


def last_kernel(gathered, mine, theirs, bias, grad_features, grad_weight, grad_bias):
    grad_features[...] = gathered[...].T.astype(BF16)
    grad_bias[...] = bias[...]
    core = lax.axis_index("col") & 1
    rows = mine.shape[0]
    for piece, half in ((mine, core), (theirs, 1 - core)):
        grad_weight[pl.ds(pl.multiple_of(half * rows, rows), rows), :] = piece[...]


def swap(value, axis, bits):
    size = lax.axis_size(axis)
    return lax.ppermute(value, axis, [(at, at ^ bits) for at in range(size)])


def dense_block(features, weight, bias, grad_out, tile_values, tile_rows, tile_cols, tile_count):
    n_row, n_col = lax.axis_size("row"), lax.axis_size("col")
    slots, tile = tile_values.shape[2:4]
    nodes, width_in = features.shape
    width_out = weight.shape[1]
    height, length = n_col * nodes, n_row * nodes
    positions = (height // tile) * (length // tile)
    whole = 2 * height * length * width_in
    shape = jax.ShapeDtypeStruct

    near = call(relay_kernel, shape(features.shape, BF16), [IN_VMEM], flops=FIRST)(swap(features, "row", 2))
    wide = 128 * pl.cdiv(max(positions, slots + 1), 128)
    lists = call(
        functools.partial(lists_kernel, length // tile), shape((2, wide), jnp.int32), [IN_VMEM, IN_VMEM, IN_SMEM], after=[near]
    )(tile_rows, tile_cols, tile_count)
    far_4, far_6 = swap(features, "row", 4), swap(features, "row", 6)
    far_4 = call(relay_kernel, shape(features.shape, BF16), [IN_VMEM], after=[lists])(far_4)
    grad_out_x = swap(grad_out, "col", 2)
    y_1, y_near = swap(features, "row", 1), swap(near, "row", 1)
    y_4, y_6 = swap(far_4, "row", 1), swap(far_6, "row", 1)
    dense = call(
        densify_kernel,
        shape((height, length), BF16),
        [IN_VMEM] * 2,
        [
            pltpu.SMEM((1, wide), jnp.int32),
            pltpu.SMEM((1, wide), jnp.int32),
            pltpu.SMEM((positions + 1,), jnp.int32),
            pltpu.SemaphoreType.DMA((2,)),
        ],
        nbytes=2 * tile_values.size * 2,
        after=[y_near],
    )(lists, tile_values.reshape(slots, tile, tile))

    def forward(parts, dtype, after=()):
        return call(
            functools.partial(forward_kernel, parts),
            shape((2 * nodes, width_in), dtype),
            [IN_VMEM] * (1 + n_row),
            flops=whole // 2,
            nbytes=height * length,
            after=after,
        )(dense, features, y_1, near, y_near, far_4, y_4, far_6, y_6)

    core_share = swap(forward((1, 3), BF16, [grad_out_x]), "col", 1)
    half = call(
        add_kernel,
        shape((2 * nodes, width_in), BF16),
        [IN_VMEM] * 2,
        nbytes=16 * nodes * width_in,
    )(forward((0, 2), F32), core_share)
    half_x = swap(half, "col", 2)
    aggregate, grad_pre, hidden, grad_aggregate = call(
        layer_kernel,
        [
            shape((2 * nodes, width_in), BF16),
            shape((2 * nodes, width_out), BF16),
            shape((nodes, width_out), BF16),
            shape((2 * nodes, width_in), BF16),
        ],
        [IN_VMEM] * 6,
        flops=8 * nodes * width_in * width_out,
        nbytes=16 * nodes * width_out,
    )(half, half_x, weight, bias.reshape(1, -1), grad_out, grad_out_x)
    grad_aggregate_core = swap(grad_aggregate, "col", 1)

    def backward(parts, dtype, after=()):
        return call(
            functools.partial(backward_kernel, parts),
            shape((len(parts), width_in, nodes), dtype),
            [IN_VMEM] * 3,
            flops=whole * len(parts) // n_row,
            nbytes=height * length * 2 * len(parts) // n_row,
            after=after,
        )(dense, grad_aggregate, grad_aggregate_core)

    mine, theirs = call(
        weight_kernel,
        [shape((width_in // 2 + 16, width_out), BF16)] * 2,
        [IN_VMEM] * 2,
        [pltpu.VMEM((width_in, width_out), F32)],
        flops=4 * nodes * width_in * width_out,
        nbytes=8 * width_in * width_out,
    )(aggregate, grad_pre)
    theirs = swap(theirs, "col", 1)

    sent_far = backward((5, 7), BF16, [theirs])
    arrived_far = swap(sent_far, "row", 1)
    sent_near = backward((2, 3), BF16, [sent_far])
    arrived_near = swap(sent_near, "row", 2)
    kept, hidden = call(
        functools.partial(kept_kernel, (4, 6, 0, 1)),
        [shape((4, width_in, nodes), F32), shape(hidden.shape, BF16)],
        [IN_VMEM] * 4,
        flops=FIRST,
        nbytes=height * length,
        after=[sent_near],
    )(dense, grad_aggregate, grad_aggregate_core, hidden)
    turned = shape((width_in, nodes), BF16)
    share_4, share_6 = call(far_kernel, [turned] * 2, [IN_VMEM] * 2, nbytes=16 * nodes * width_in)(
        kept, arrived_far
    )

    def merge(own, other, after=()):
        return call(
            functools.partial(merge_kernel, width_in // 2),
            shape(own.shape, BF16),
            [IN_VMEM] * 2,
            nbytes=6 * own.size,
            after=after,
        )(own, other)

    part = merge(mine, theirs, [sent_far])
    part = merge(part, swap(part, "row", 4), [kept])
    part = merge(part, swap(part, "row", 2))
    near = call(
        near_kernel,
        shape((width_in + part.shape[0], nodes), BF16),
        [IN_VMEM] * 3,
        nbytes=8 * nodes * width_in,
    )(kept, arrived_near, part)
    near = swap(near, "row", 1)
    half_weight, bias_sum = call(
        last_merge_kernel,
        [shape((width_in // 2, width_out), F32), shape((1, width_out), F32)],
        [IN_VMEM] * 2,
        nbytes=8 * part.size,
    )(part, near)
    turned = shape((width_in, nodes), F32)
    gathered = call(gather_far_kernel, turned, [IN_VMEM] * 2, flops=SOON)(kept, swap(share_4, "row", 4))
    gathered = call(gather_near_kernel, turned, [IN_VMEM] * 3)(arrived_near, near, gathered)
    gathered = call(gather_last_kernel, turned, [IN_VMEM] * 2, flops=FIRST)(swap(share_6, "row", 6), gathered)
    grad_features, grad_weight, grad_bias = call(
        last_kernel,
        [
            shape((nodes, width_in), BF16),
            shape((width_in, width_out), F32),
            shape((1, width_out), F32),
        ],
        [IN_VMEM] * 4,
        nbytes=16 * nodes * width_in,
    )(gathered, half_weight, swap(half_weight, "col", 1), bias_sum)
    return hidden, grad_weight, grad_bias.reshape(-1), grad_features


def sparse_block(features, weight, bias, grad_out, tile_values, tile_rows, tile_cols, tile_count):
    values = tile_values[0, 0]
    slot_rows = tile_rows[0, 0]
    slot_cols = tile_cols[0, 0]
    tile_size = values.shape[1]
    width_in = features.shape[1]
    node_rows = features.shape[0]
    live = (jnp.arange(values.shape[0]) < tile_count[0, 0]).astype(values.dtype)
    values = values * live[:, None, None]
    panel = lax.all_gather(features, "row", axis=0, tiled=True)
    panel_tiles = panel.reshape(-1, tile_size, width_in)
    picked = panel_tiles[slot_cols]
    products = jnp.einsum("kij,kjf->kif", values, picked, preferred_element_type=F32)
    row_segments = lax.axis_size("col") * node_rows // tile_size
    partial_value = jax.ops.segment_sum(products, slot_rows, num_segments=row_segments).reshape(
        -1, width_in
    )
    aggregate = lax.psum_scatter(
        partial_value.astype(BF16), "col", scatter_dimension=0, tiled=True
    )
    preact = jnp.dot(aggregate, weight, preferred_element_type=F32) + bias
    sigmoid_pre = jax.nn.sigmoid(preact)
    hidden = (preact * sigmoid_pre).astype(BF16)
    slope_factor = sigmoid_pre * (1.0 + preact * (1.0 - sigmoid_pre))
    grad_pre = (grad_out.astype(F32) * slope_factor).astype(BF16)
    local_weight = jnp.dot(aggregate.T, grad_pre, preferred_element_type=F32)
    local_bias = jnp.sum(grad_pre.astype(F32), axis=0)
    grad_weight, grad_bias = lax.psum((local_weight, local_bias), ("row", "col"))
    grad_aggregate = jnp.dot(grad_pre, weight.T, preferred_element_type=F32).astype(BF16)
    block_aggregate = lax.all_gather(grad_aggregate, "col", axis=0, tiled=True)
    block_tiles = block_aggregate.reshape(-1, tile_size, width_in)
    picked_back = block_tiles[slot_rows]
    back_products = jnp.einsum(
        "kji,kjf->kif", values, picked_back, preferred_element_type=F32
    )
    col_segments = lax.axis_size("row") * node_rows // tile_size
    partial_back = jax.ops.segment_sum(back_products, slot_cols, num_segments=col_segments).reshape(
        -1, width_in
    )
    grad_features = lax.psum_scatter(
        partial_back.astype(BF16), "row", scatter_dimension=0, tiled=True
    )
    return hidden, grad_weight, grad_bias, grad_features


def per_device(features, weight, bias, grad_out, tile_values, tile_rows, tile_cols, tile_count):
    n_row, n_col = lax.axis_size("row"), lax.axis_size("col")
    slots, tile = tile_values.shape[2:4]
    nodes = features.shape[0]
    positions = n_row * n_col * (nodes // tile) ** 2
    block = dense_block if (n_row, n_col) == (8, 4) and positions <= 2 * slots else sparse_block
    return block(features, weight, bias, grad_out, tile_values, tile_rows, tile_cols, tile_count)


def solution(mesh):
    return jax.shard_map(
        per_device,
        mesh=mesh,
        in_specs=(
            P(("col", "row"), None),
            P(),
            P(),
            P(("row", "col"), None),
            P("row", "col", None, None, None),
            P("row", "col", None),
            P("row", "col", None),
            P("row", "col"),
        ),
        out_specs=(P(("row", "col"), None), P(), P(), P(("col", "row"), None)),
        check_vma=False,
    )
```
